32 devices in a mesh: samp: 4 (over z), slab: 4 (over x, core), chan: 2 (over y).
Axes of the slice: x: 2, y: 2, z: 4, core: 2. Of those that a mesh axis runs over, the one named last changes fastest.
Arguments:
- volume: bfloat16 [4, 128, 8, 1024], P('samp', 'chan', 'slab'), may hold values from -6 to 6
- cotangent: bfloat16 [4, 128, 8, 1024], P('samp', 'chan', 'slab'), may hold values from -6 to 6
- filter_one: bfloat16 [128, 27, 128], P('chan'), may hold values from -0.109375 to 0.109375
- filter_two: bfloat16 [128, 27, 128], P('chan'), may hold values from -0.109375 to 0.109375
Outputs:
- block_out: bfloat16 [4, 128, 8, 1024], P('samp', 'chan', 'slab')
- grad_volume: bfloat16 [4, 128, 8, 1024], P('samp', 'chan', 'slab')
- grad_filter_one: float32 [128, 27, 128], P('chan')
- grad_filter_two: float32 [128, 27, 128], P('chan')
The draws below stay inside these ranges and needn't reach their ends.
All inputs are finite; a program needn't handle non-finite values.
Results may differ from the reference program's by a relative error of at most 0.0033.
Values may be sent and summed in bfloat16 or wider, within the bound.
A program may use at most 64 MiB of HBM per device.

```python
import math
import jax
import jax.numpy as jnp

C = 128
SIDE = 32
SAMPLES = 4
DEPTH = 8


def block_levels(key, dims, split, low, top_value):
    loudness = 1.0
    for dim, shards_of in split:
        steps = jax.random.uniform(jax.random.fold_in(jax.random.fold_in(key, 6), dim), (shards_of,), jnp.float32, low / len(split), top_value / len(split))
        loudness = loudness * jnp.repeat(jnp.exp(steps), dims[dim] // shards_of).reshape((-1,) + (1,) * (len(dims) - 1 - dim))
    return loudness


def normal_values(stream_key, extent, scale, bound, cuts=(), dtype=jnp.bfloat16):
    factor_of = block_levels(stream_key, extent, cuts, -0.22, 0.18) if cuts else 1.0
    entries = jax.random.normal(stream_key, extent, jnp.float32) * scale * factor_of
    return jnp.minimum(jnp.maximum(entries, -bound), bound).astype(dtype)


def setup_inputs(seed: int = 0) -> dict:
    seeds = jax.random.split(jax.random.key(seed), 5)
    volume = normal_values(seeds[0], (SAMPLES, C, DEPTH, SIDE * SIDE), 1.0, 6.0, ((0, 4), (1, 2), (2, 4)))
    cotangent = normal_values(seeds[1], (SAMPLES, C, DEPTH, SIDE * SIDE), 1.0, 6.0, ((0, 4), (1, 2), (2, 4)))
    filter_one = normal_values(seeds[2], (C, 27, C), (27 * C) ** -0.5, 0.109375, ((0, 2),))
    filter_two = normal_values(seeds[3], (C, 27, C), (27 * C) ** -0.5, 0.109375, ((0, 2),))
    return {"volume": volume, "cotangent": cotangent, "filter_one": filter_one, "filter_two": filter_two}


plane_offsets = [(-1, -1), (-1, 0), (-1, 1), (0, -1), (0, 0), (0, 1), (1, -1), (1, 0), (1, 1)]

def plane_shift(values, row_off, col_off):
    length = values.shape[-1]
    widths = [(0, 0)] * (values.ndim - 1) + [(SIDE + 1, SIDE + 1)]
    padded = jnp.pad(values, widths)
    begin_at = SIDE + 1 + row_off * SIDE + col_off
    shifted_flat = padded[..., begin_at:begin_at + length]
    column = jnp.arange(length) % SIDE + col_off
    inside = (column >= 0) & (column < SIDE)
    return jnp.where(inside, shifted_flat, jnp.zeros_like(shifted_flat))

def convolve(padded, weight):
    out_count, tap_count, in_count = weight.shape
    planes = padded.shape[1] - 2
    shifted = jnp.stack([plane_shift(padded, row_off, col_off) for row_off, col_off in plane_offsets]).astype(jnp.float32)
    blocks = weight.reshape(out_count, 3, 9, in_count).astype(jnp.float32)
    summed = jnp.zeros((out_count, planes, padded.shape[2]), jnp.float32)
    for depth_off in range(3):
        summed = summed + jnp.einsum('ojn,jndp->odp', blocks[:, depth_off], shifted[:, :, depth_off:depth_off + planes])
    return summed

def filter_grad(gradient, padded):
    out_count, planes, inner = gradient.shape
    shifted = jnp.stack([plane_shift(gradient, -row_off, -col_off) for row_off, col_off in plane_offsets]).astype(jnp.float32)
    wide = padded.astype(jnp.float32)
    pieces = [jnp.einsum('jodp,ndp->ojn', shifted, wide[:, depth_off:depth_off + planes]) for depth_off in range(3)]
    return jnp.stack(pieces, axis=1).reshape(out_count, 27, padded.shape[0])

def reverse_filter(weight):
    return jnp.transpose(weight[:, ::-1, :], (2, 1, 0))

def depth_pad(values):
    return jnp.pad(values, ((0, 0), (1, 1), (0, 0)))

def reference(volume, cotangent, filter_one, filter_two):
    norm_scale = 1.0 / math.sqrt(SAMPLES * DEPTH * SIDE * SIDE)
    results = []
    grads = []
    grad_one = jnp.zeros((C, 27, C), jnp.float32)
    grad_two = jnp.zeros((C, 27, C), jnp.float32)
    for sample_idx in range(SAMPLES):
        source = volume[sample_idx]
        upstream = cotangent[sample_idx]
        source_pad = depth_pad(source)
        pre_one = convolve(source_pad, filter_one)
        hidden = (pre_one * jax.nn.sigmoid(pre_one)).astype(jnp.bfloat16)
        hidden_pad = depth_pad(hidden)
        pre_two = convolve(hidden_pad, filter_two)
        results.append((source.astype(jnp.float32) + pre_two).astype(jnp.bfloat16))
        grad_two = grad_two + filter_grad(upstream, hidden_pad)
        grad_hidden = convolve(depth_pad(upstream), reverse_filter(filter_two))
        sigma = jax.nn.sigmoid(pre_one)
        grad_pre = (grad_hidden * sigma * (1.0 + pre_one * (1.0 - sigma))).astype(jnp.bfloat16)
        grad_one = grad_one + filter_grad(grad_pre, source_pad)
        back = convolve(depth_pad(grad_pre), reverse_filter(filter_one))
        grads.append((upstream.astype(jnp.float32) + back).astype(jnp.bfloat16))
    return (jnp.stack(results), jnp.stack(grads), grad_one * norm_scale, grad_two * norm_scale)
```

```python
import functools
import math

import jax
import jax.numpy as jnp
from jax import lax
from jax.experimental import pallas as pl
from jax.experimental.pallas import tpu as pltpu
from jax.sharding import PartitionSpec as P

SIDE = 32
CELLS = SIDE * SIDE
TILE = 512
MESH = pl.DeviceIdType.MESH
F32 = jnp.float32
BF16 = jnp.bfloat16

plane_offsets = [(-1, -1), (-1, 0), (-1, 1), (0, -1), (0, 0), (0, 1), (1, -1), (1, 0), (1, 1)]
SUM_TYPES = (F32, BF16)


def kernel(sizes, x_ref, ct_ref, w1_ref, w2_ref, w1t_ref, w2t_ref,
           out_ref, gv_ref, q1_ref, q2_ref,
           xpad, hpad, ctpad, gppad, wide, st_ct, st_gp, pre, gh, back,
           part_out, part_in, back_out, back_in,
           g1, g2, s1_1, r1_1, s2_1, r2_1, s1_2, r1_2, s2_2, r2_2,
           sx, rx, sxh, rxh, sct, rct, sgh, rgh, sh, rh, shh, rhh, sgp, rgp, sbk, rbk, sred, rred):
    nz, ns, nc, n, planes, shard, piece, norm_scale = sizes
    channels = n * nc
    zi, si, ci = lax.axis_index("samp"), lax.axis_index("slab"), lax.axis_index("chan")
    has_low, has_high = si > 0, si < ns - 1

    barrier = pltpu.get_barrier_semaphore()
    for k in range(1, nc):
        pl.semaphore_signal(barrier, inc=1, device_id={"chan": lax.rem(ci + k, nc)}, device_id_type=MESH)
    for k in range(1, ns):
        pl.semaphore_signal(barrier, inc=1, device_id={"slab": lax.rem(si + k, ns)}, device_id_type=MESH)
    for k in range(1, nz):
        pl.semaphore_signal(barrier, inc=1, device_id={"samp": lax.rem(zi + k, nz)}, device_id_type=MESH)
    pl.semaphore_wait(barrier, nc + ns + nz - 3)

    def rows_of(index):
        return pl.ds(pl.multiple_of(index * n, n), n)

    def send(src, dst, send_sem, recv_sem, axis, index):
        return pltpu.make_async_remote_copy(
            src_ref=src, dst_ref=dst, send_sem=send_sem, recv_sem=recv_sem,
            device_id={axis: index}, device_id_type=MESH)

    def halo_sends(padded, rows, ssem, rsem, slot):
        low = send(padded.at[1, rows], padded.at[planes + 1, rows], ssem.at[2 * slot], rsem.at[2 * slot], "slab", si - 1)
        high = send(padded.at[planes, rows], padded.at[0, rows], ssem.at[2 * slot + 1], rsem.at[2 * slot + 1], "slab", si + 1)
        return low, high

    def start_halo(*args):
        low, high = halo_sends(*args)
        pl.when(has_low)(low.start)
        pl.when(has_high)(high.start)

    def wait_halo(*args):
        low, high = halo_sends(*args)
        pl.when(has_high)(low.wait_recv)
        pl.when(has_low)(high.wait_recv)

    def finish_halo(*args):
        low, high = halo_sends(*args)
        pl.when(has_low)(low.wait_send)
        pl.when(has_high)(high.wait_send)

    own = rows_of(ci)
    everything = pl.ds(0, n)
    inside = pl.ds(1, planes)

    def gather_sends(padded, ssem, rsem):
        return [send(padded.at[inside, own], padded.at[inside, own], ssem.at[k - 1], rsem.at[k - 1],
                     "chan", lax.rem(ci + k, nc)) for k in range(1, nc)]

    def gather_arrivals(padded, ssem, rsem):
        out = []
        for k in range(1, nc):
            rows = rows_of(lax.rem(ci + nc - k, nc))
            out.append((k, rows, send(padded.at[inside, rows], padded.at[inside, rows], ssem.at[k - 1],
                                      rsem.at[k - 1], "chan", lax.rem(ci + k, nc))))
        return out

    def zero_edges(padded):
        @pl.when(jnp.logical_not(has_low))
        def _():
            padded[0] = jnp.zeros(padded.shape[1:], BF16)

        @pl.when(jnp.logical_not(has_high))
        def _():
            padded[planes + 1] = jnp.zeros(padded.shape[1:], BF16)

    cell = lax.broadcasted_iota(jnp.int32, (1, CELLS), 1)
    row, column = cell // SIDE, cell % SIDE
    masks = []
    for b, c in plane_offsets:
        ok = (row + b >= 0) & (row + b < SIDE) & (column + c >= 0) & (column + c < SIDE)
        masks.append(jnp.where(ok, 1.0, 0.0).astype(F32))

    def build(stack, padded, plane):
        count = padded.shape[1]

        def body(step, _):
            start = pl.multiple_of(step * 16, 16)
            values = padded[plane, pl.ds(start, 16), :]
            wide_values = values.astype(F32)
            for j, (b, c) in enumerate(plane_offsets):
                shift = (-(SIDE * b + c)) % CELLS
                if shift == 0:
                    moved = values
                else:
                    moved = (pltpu.roll(wide_values, shift, 1) * masks[j]).astype(BF16)
                stack[plane, pl.ds(pl.multiple_of(j * count + step * 16, 16), 16), :] = moved
            return 0

        lax.fori_loop(0, count // 16, body, 0)

    def convolve(weight, stack, emit):
        tiles = CELLS // TILE

        def body(step, _):
            d = step // tiles
            cols = pl.ds(pl.multiple_of((step % tiles) * TILE, TILE), TILE)
            total = None
            for a in range(3):
                term = jnp.dot(weight(a), stack[d + a, :, cols], preferred_element_type=F32)
                total = term if total is None else total + term
            emit(d, cols, total)
            return 0

        lax.fori_loop(0, planes * tiles, body, 0)

    def filter_grad(total_ref, stack, padded):
        count = stack.shape[1]
        for a in range(3):
            total = None
            for d in range(planes):
                term = lax.dot_general(stack[d + 1], padded[d + a], (((1,), (1,)), ((), ())),
                                       preferred_element_type=F32)
                total = term if total is None else total + term
            total_ref[pl.ds(a * count, count), :] = total
        rest = ns * shard - 3 * count
        if rest:
            total_ref[pl.ds(3 * count, rest), :] = jnp.zeros((rest, channels), F32)

    xpad[inside, own, :] = x_ref[...]
    for copy in gather_sends(xpad, sx, rx):
        copy.start()
    start_halo(xpad, own, sxh, rxh, 0)
    ctpad[inside] = ct_ref[...]
    start_halo(ctpad, everything, sct, rct, 0)

    zero_edges(ctpad)
    zero_edges(xpad)
    for plane in range(1, planes + 1):
        build(st_ct, ctpad, plane)
    wait_halo(ctpad, everything, sct, rct, 0)
    build(st_ct, ctpad, 0)
    build(st_ct, ctpad, planes + 1)

    def reverse_parts(weight_t, stack, mine, outgoing, incoming, ssem, rsem):
        for k in range(1, nc):
            target = lax.rem(ci + k, nc)

            def emit(d, cols, total, k=k):
                outgoing[k - 1, d, :, cols] = total.astype(outgoing.dtype)

            convolve(lambda a: weight_t[a, rows_of(target), :], stack, emit)
            send(outgoing.at[k - 1], incoming.at[k - 1], ssem.at[k - 1], rsem.at[k - 1], "chan", target).start()

        def keep(d, cols, total):
            mine[d, :, cols] = total

        convolve(lambda a: weight_t[a, own, :], stack, keep)

    def part_copies(outgoing, incoming, ssem, rsem):
        return [send(outgoing.at[k - 1], incoming.at[k - 1], ssem.at[k - 1], rsem.at[k - 1],
                     "chan", lax.rem(ci + k, nc)) for k in range(1, nc)]

    reverse_parts(w2t_ref, st_ct, gh, part_out, part_in, sgh, rgh)

    for k, rows, copy in gather_arrivals(xpad, sx, rx):
        copy.wait_recv()
        start_halo(xpad, rows, sxh, rxh, k)
    for plane in range(1, planes + 1):
        build(wide, xpad, plane)
    for k in range(nc):
        wait_halo(xpad, rows_of(lax.rem(ci + nc - k, nc)), sxh, rxh, k)
    build(wide, xpad, 0)
    build(wide, xpad, planes + 1)

    def hidden_out(d, cols, total):
        pre[d, :, cols] = total
        hpad[d + 1, own, cols] = (total * jax.nn.sigmoid(total)).astype(BF16)

    convolve(lambda a: w1_ref[a], wide, hidden_out)
    for copy in gather_sends(hpad, sh, rh):
        copy.start()
    start_halo(hpad, own, shh, rhh, 0)
    zero_edges(hpad)
    zero_edges(gppad)

    for copy in part_copies(part_out, part_in, sgh, rgh):
        copy.wait_recv()

    def slope(step, _):
        d = step // (n // 16)
        rows = pl.ds(pl.multiple_of((step % (n // 16)) * 16, 16), 16)
        total = gh[d, rows, :]
        for k in range(nc - 1):
            total = total + part_in[k, d, rows, :].astype(F32)
        values = pre[d, rows, :]
        sigma = jax.nn.sigmoid(values)
        gppad[d + 1, rows, :] = (total * (sigma * (1.0 + values * (1.0 - sigma)))).astype(BF16)
        return 0

    lax.fori_loop(0, planes * (n // 16), slope, 0)
    start_halo(gppad, everything, sgp, rgp, 0)
    for plane in range(1, planes + 1):
        build(st_gp, gppad, plane)
    filter_grad(g1, st_gp, xpad)

    def shard_rows(index):
        return pl.ds(pl.multiple_of(index * shard, 16), shard)

    def piece_rows(slab_index, samp_index):
        return pl.ds(pl.multiple_of(slab_index * shard + samp_index * piece, 16), piece)

    class Reduction:
        def __init__(self, which, total, out1, in1, out2, in2, result):
            self.total, self.out1, self.in1, self.out2, self.in2, self.result = total, out1, in1, out2, in2, result
            base = which * 2 * (ns + nz)
            self.base1, self.base2 = base, base + ns
            self.base3, self.base4 = base + ns + nz, base + ns + 2 * nz

        def slab_copies(self):
            return [send(self.out1.at[k - 1], self.in1.at[k - 1], sred.at[self.base1 + k], rred.at[self.base1 + k],
                         "slab", lax.rem(si + k, ns)) for k in range(1, ns)]

        def samp_copies(self):
            return [send(self.out2.at[k - 1], self.in2.at[k - 1], sred.at[self.base2 + k], rred.at[self.base2 + k],
                         "samp", lax.rem(zi + k, nz)) for k in range(1, nz)]

        def samp_gather(self, back_by):
            out = []
            for k in range(1, nz):
                rows = piece_rows(si, lax.rem(zi + nz - k, nz) if back_by else zi)
                out.append(send(self.result.at[rows], self.result.at[rows], sred.at[self.base3 + k],
                                rred.at[self.base3 + k], "samp", lax.rem(zi + k, nz)))
            return out

        def slab_gather(self, back_by):
            out = []
            for k in range(1, ns):
                rows = shard_rows(lax.rem(si + ns - k, ns) if back_by else si)
                out.append(send(self.result.at[rows], self.result.at[rows], sred.at[self.base4 + k],
                                rred.at[self.base4 + k], "slab", lax.rem(si + k, ns)))
            return out

        def one(self):
            copies = self.slab_copies()
            for k in range(1, ns):
                rows = shard_rows(lax.rem(si + k, ns))
                self.out1[k - 1] = self.total[rows, :].astype(self.out1.dtype)
                copies[k - 1].start()

        def two(self):
            for copy in self.slab_copies():
                copy.wait_recv()
            rows = shard_rows(si)
            summed = self.total[rows, :]
            for k in range(ns - 1):
                summed = summed + self.in1[k].astype(F32)
            self.total[rows, :] = summed
            copies = self.samp_copies()
            for k in range(1, nz):
                self.out2[k - 1] = self.total[piece_rows(si, lax.rem(zi + k, nz)), :].astype(self.out2.dtype)
                copies[k - 1].start()

        def three(self):
            for copy in self.samp_copies():
                copy.wait_recv()
            rows = piece_rows(si, zi)
            summed = self.total[rows, :]
            for k in range(nz - 1):
                summed = summed + self.in2[k].astype(F32)
            self.result[rows, :] = (summed * norm_scale).astype(BF16)
            for copy in self.samp_gather(False):
                copy.start()

        def four(self):
            for copy in self.samp_gather(True):
                copy.wait_recv()
            for copy in self.slab_gather(False):
                copy.start()

        def five(self):
            for copy in self.slab_gather(True):
                copy.wait_recv()

        def finish(self):
            for copy in self.slab_copies() + self.samp_copies() + self.samp_gather(False) + self.slab_gather(False):
                copy.wait_send()

    first = Reduction(0, g1, s1_1, r1_1, s2_1, r2_1, q1_ref)
    second = Reduction(1, g2, s1_2, r1_2, s2_2, r2_2, q2_ref)
    first.one()

    wait_halo(gppad, everything, sgp, rgp, 0)
    build(st_gp, gppad, 0)
    build(st_gp, gppad, planes + 1)
    reverse_parts(w1t_ref, st_gp, back, back_out, back_in, sbk, rbk)

    for k, rows, copy in gather_arrivals(hpad, sh, rh):
        copy.wait_recv()
        start_halo(hpad, rows, shh, rhh, k)
    first.two()
    for plane in range(1, planes + 1):
        build(wide, hpad, plane)
    for k in range(nc):
        wait_halo(hpad, rows_of(lax.rem(ci + nc - k, nc)), shh, rhh, k)
    filter_grad(g2, st_ct, hpad)
    second.one()
    first.three()
    build(wide, hpad, 0)
    build(wide, hpad, planes + 1)

    def block(d, cols, total):
        out_ref[d, :, cols] = (x_ref[d, :, cols].astype(F32) + total).astype(BF16)

    convolve(lambda a: w2_ref[a], wide, block)
    second.two()
    first.four()

    for copy in part_copies(back_out, back_in, sbk, rbk):
        copy.wait_recv()

    def volume_grad(step, _):
        d = step // (n // 16)
        rows = pl.ds(pl.multiple_of((step % (n // 16)) * 16, 16), 16)
        total = back[d, rows, :]
        for k in range(nc - 1):
            total = total + back_in[k, d, rows, :].astype(F32)
        gv_ref[d, rows, :] = (ct_ref[d, rows, :].astype(F32) + total).astype(BF16)
        return 0

    lax.fori_loop(0, planes * (n // 16), volume_grad, 0)
    second.three()
    second.four()
    first.five()
    second.five()

    for copy in gather_sends(xpad, sx, rx) + gather_sends(hpad, sh, rh):
        copy.wait_send()
    for copy in part_copies(part_out, part_in, sgh, rgh) + part_copies(back_out, back_in, sbk, rbk):
        copy.wait_send()
    for k in range(nc):
        rows = rows_of(lax.rem(ci + nc - k, nc))
        finish_halo(xpad, rows, sxh, rxh, k)
        finish_halo(hpad, rows, shh, rhh, k)
    finish_halo(ctpad, everything, sct, rct, 0)
    finish_halo(gppad, everything, sgp, rgp, 0)
    first.finish()
    second.finish()


def per_device(volume, cotangent, filter_one, filter_two):
    n, planes, cells = volume.shape[1:]
    nz, ns, nc = (lax.axis_size(axis) for axis in ("samp", "slab", "chan"))
    channels = n * nc
    norm_scale = 1.0 / math.sqrt(nz * planes * ns * cells)
    unit = 16 * ns * nz
    rows = -(-27 * n // unit) * unit
    shard, piece = rows // ns, rows // ns // nz

    def forward(weight):
        return jnp.transpose(weight.reshape(n, 3, 9 * channels), (1, 0, 2))

    def backward(weight):
        flipped = weight[:, ::-1, :].reshape(n, 3, 9, channels)
        return jnp.transpose(flipped, (1, 3, 2, 0)).reshape(3, channels, 9 * n)

    x = jnp.transpose(volume[0], (1, 0, 2))
    ct = jnp.transpose(cotangent[0], (1, 0, 2))
    vmem = pl.BlockSpec(memory_space=pltpu.VMEM)
    padded = planes + 2
    dma = pltpu.SemaphoreType.DMA

    def reduction_buffers(dtype):
        return [pltpu.VMEM((ns - 1, shard, channels), dtype)] * 2 + [pltpu.VMEM((nz - 1, piece, channels), dtype)] * 2

    scratch = [
        pltpu.VMEM((padded, channels, cells), BF16),
        pltpu.VMEM((padded, channels, cells), BF16),
        pltpu.VMEM((padded, n, cells), BF16),
        pltpu.VMEM((padded, n, cells), BF16),
        pltpu.VMEM((padded, 9 * channels, cells), BF16),
        pltpu.VMEM((padded, 9 * n, cells), BF16),
        pltpu.VMEM((padded, 9 * n, cells), BF16),
        pltpu.VMEM((planes, n, cells), F32),
        pltpu.VMEM((planes, n, cells), F32),
        pltpu.VMEM((planes, n, cells), F32),
    ] + [pltpu.VMEM((nc - 1, planes, n, cells), BF16)] * 4 + [
        pltpu.VMEM((rows, channels), F32),
        pltpu.VMEM((rows, channels), F32),
    ] + reduction_buffers(SUM_TYPES[0]) + reduction_buffers(SUM_TYPES[1]) + [
        dma((nc,)), dma((nc,)), dma((2 * nc,)), dma((2 * nc,)),
        dma((2,)), dma((2,)), dma((nc,)), dma((nc,)),
        dma((nc,)), dma((nc,)), dma((2 * nc,)), dma((2 * nc,)),
        dma((2,)), dma((2,)), dma((nc,)), dma((nc,)),
        dma((4 * (ns + nz),)), dma((4 * (ns + nz),)),
    ]
    sizes = (nz, ns, nc, n, planes, shard, piece, norm_scale)
    block, grad_volume, one, two = pl.pallas_call(
        functools.partial(kernel, sizes),
        out_shape=(
            jax.ShapeDtypeStruct((planes, n, cells), BF16),
            jax.ShapeDtypeStruct((planes, n, cells), BF16),
            jax.ShapeDtypeStruct((rows, channels), BF16),
            jax.ShapeDtypeStruct((rows, channels), BF16),
        ),
        in_specs=[vmem] * 6,
        out_specs=(vmem,) * 4,
        scratch_shapes=scratch,
        compiler_params=pltpu.CompilerParams(
            collective_id=0, has_side_effects=True, vmem_limit_bytes=56 * 1024 * 1024),
        cost_estimate=pl.CostEstimate(
            flops=6 * 2 * planes * cells * n * 27 * channels, bytes_accessed=8 << 20, transcendentals=planes * n * cells),
        name="residual_pair",
    )(x, ct, forward(filter_one), forward(filter_two), backward(filter_one), backward(filter_two))

    def filter_out(values):
        values = values[: 27 * n].reshape(3, 9, n, channels)[:, ::-1]
        return jnp.transpose(values, (2, 0, 1, 3)).reshape(n, 27, channels).astype(F32)

    return (
        jnp.transpose(block, (1, 0, 2))[None],
        jnp.transpose(grad_volume, (1, 0, 2))[None],
        filter_out(one),
        filter_out(two),
    )


def solution(mesh):
    return jax.shard_map(
        per_device,
        mesh=mesh,
        in_specs=(
            P("samp", "chan", "slab", None),
            P("samp", "chan", "slab", None),
            P("chan", None, None),
            P("chan", None, None),
        ),
        out_specs=(
            P("samp", "chan", "slab", None),
            P("samp", "chan", "slab", None),
            P("chan", None, None),
            P("chan", None, None),
        ),
        check_vma=False,
    )
```

```python
import functools
import math

import jax
import jax.numpy as jnp
from jax import lax
from jax.experimental import pallas as pl
from jax.experimental.pallas import tpu as pltpu
from jax.sharding import PartitionSpec as P

SIDE = 32
CELLS = SIDE * SIDE
TILE = 256
MESH = pl.DeviceIdType.MESH
F32 = jnp.float32
BF16 = jnp.bfloat16

plane_offsets = [(-1, -1), (-1, 0), (-1, 1), (0, -1), (0, 0), (0, 1), (1, -1), (1, 0), (1, 1)]
SUM_TYPES = ((F32, F32, F32), (BF16, BF16, BF16))


def kernel(sizes, x_ref, ct_ref, w1_ref, w2_ref, w1t_ref, w2t_ref,
           out_ref, gv_ref, q1_ref, q2_ref,
           xpad, hpad, ctpad, gppad, wide, st_ct, st_gp, pre, gh, back,
           part_out, part_in, back_out, back_in,
           g1, g2, sums1, sums2,
           sx, rx, sxh, rxh, sct, rct, sgh, rgh, sh, rh, shh, rhh, sgp, rgp, sbk, rbk, sred, rred):
    nz, ns, nc, n, planes, shard, piece, norm_scale = sizes
    channels = n * nc
    zi, si, ci = lax.axis_index("samp"), lax.axis_index("slab"), lax.axis_index("chan")
    has_low, has_high = si > 0, si < ns - 1

    barrier = pltpu.get_barrier_semaphore()
    for k in range(1, nc):
        pl.semaphore_signal(barrier, inc=1, device_id={"chan": lax.rem(ci + k, nc)}, device_id_type=MESH)
    for k in range(1, ns):
        pl.semaphore_signal(barrier, inc=1, device_id={"slab": lax.rem(si + k, ns)}, device_id_type=MESH)
    for k in range(1, nz):
        pl.semaphore_signal(barrier, inc=1, device_id={"samp": lax.rem(zi + k, nz)}, device_id_type=MESH)
    pl.semaphore_wait(barrier, nc + ns + nz - 3)

    def rows_of(index):
        return pl.ds(pl.multiple_of(index * n, n), n)

    def send(src, dst, send_sem, recv_sem, axis, index):
        return pltpu.make_async_remote_copy(
            src_ref=src, dst_ref=dst, send_sem=send_sem, recv_sem=recv_sem,
            device_id={axis: index}, device_id_type=MESH)

    def halo_sends(padded, rows, ssem, rsem, slot):
        low = send(padded.at[1, rows], padded.at[planes + 1, rows], ssem.at[2 * slot], rsem.at[2 * slot], "slab", si - 1)
        high = send(padded.at[planes, rows], padded.at[0, rows], ssem.at[2 * slot + 1], rsem.at[2 * slot + 1], "slab", si + 1)
        return low, high

    def start_halo(*args):
        low, high = halo_sends(*args)
        pl.when(has_low)(low.start)
        pl.when(has_high)(high.start)

    def wait_halo(*args):
        low, high = halo_sends(*args)
        pl.when(has_high)(low.wait_recv)
        pl.when(has_low)(high.wait_recv)

    def finish_halo(*args):
        low, high = halo_sends(*args)
        pl.when(has_low)(low.wait_send)
        pl.when(has_high)(high.wait_send)

    own = rows_of(ci)
    everything = pl.ds(0, n)
    inside = pl.ds(1, planes)

    def gather_sends(padded, ssem, rsem):
        return [send(padded.at[1 + d, own], padded.at[1 + d, own], ssem.at[planes * (k - 1) + d],
                     rsem.at[planes * (k - 1) + d], "chan", lax.rem(ci + k, nc))
                for d in range(planes) for k in range(1, nc)]

    def gather_and_forward(padded, ssem, rsem, fsend, frecv):
        for d in range(planes):
            for k in range(1, nc):
                rows = rows_of(lax.rem(ci + nc - k, nc))
                at = planes * (k - 1) + d
                send(padded.at[1 + d, rows], padded.at[1 + d, rows], ssem.at[at], rsem.at[at],
                     "chan", lax.rem(ci + k, nc)).wait_recv()
                low, high = halo_sends(padded, rows, fsend, frecv, k)
                if d == 0:
                    pl.when(has_low)(low.start)
                if d == planes - 1:
                    pl.when(has_high)(high.start)

    def zero_edges(padded):
        @pl.when(jnp.logical_not(has_low))
        def _():
            padded[0] = jnp.zeros(padded.shape[1:], BF16)

        @pl.when(jnp.logical_not(has_high))
        def _():
            padded[planes + 1] = jnp.zeros(padded.shape[1:], BF16)

    cell = lax.broadcasted_iota(jnp.int32, (1, CELLS), 1)
    row, column = cell // SIDE, cell % SIDE
    masks = []
    for b, c in plane_offsets:
        ok = (row + b >= 0) & (row + b < SIDE) & (column + c >= 0) & (column + c < SIDE)
        masks.append(jnp.broadcast_to(jnp.where(ok, 1.0, 0.0).astype(BF16), (16, CELLS)))

    def build(stack, padded, plane, sign=1):
        count = padded.shape[1]

        def body(step, _):
            start = pl.multiple_of(step * 16, 16)
            values = padded[plane, pl.ds(start, 16), :]
            for j, (b, c) in enumerate(plane_offsets):
                shift = (-sign * (SIDE * b + c)) % CELLS
                if shift == 0:
                    moved = values
                else:
                    moved = pltpu.roll(values, shift, 1) * masks[j if sign > 0 else 8 - j]
                stack[plane, pl.ds(pl.multiple_of(j * count + step * 16, 16), 16), :] = moved
            return 0

        lax.fori_loop(0, count // 16, body, 0)

    def convolve(weight, stack, emit, reverse=False):
        def body(step, _):
            cols = pl.ds(pl.multiple_of(step * TILE, TILE), TILE)
            totals = [None] * planes
            for p in range(planes + 2):
                pairs = []
                for d in range(planes):
                    a = d + 2 - p if reverse else p - d
                    if 0 <= a < 3:
                        pairs.append((d, a))
                left = jnp.concatenate([weight[a] for _, a in pairs], axis=0)
                term = jnp.dot(left, stack[p, :, cols], preferred_element_type=F32)
                height = weight.shape[1]
                for at, (d, _) in enumerate(pairs):
                    part = term[at * height : (at + 1) * height]
                    totals[d] = part if totals[d] is None else totals[d] + part
            for d in range(planes):
                emit(d, cols, totals[d])
            return 0

        lax.fori_loop(0, CELLS // TILE, body, 0)

    def filter_grad(total_ref, stack, padded):
        count = stack.shape[1]
        for a in range(3):
            total = None
            for d in range(planes):
                term = lax.dot_general(stack[d + 1], padded[d + a], (((1,), (1,)), ((), ())),
                                       preferred_element_type=F32)
                total = term if total is None else total + term
            total_ref[pl.ds(a * count, count), :] = total
        rest = ns * shard - 3 * count
        if rest:
            total_ref[pl.ds(3 * count, rest), :] = jnp.zeros((rest, channels), F32)

    xpad[inside, own, :] = x_ref[...]
    for copy in gather_sends(xpad, sx, rx):
        copy.start()
    start_halo(xpad, own, sxh, rxh, 0)
    ctpad[inside] = ct_ref[...]
    start_halo(ctpad, everything, sct, rct, 0)

    zero_edges(ctpad)
    zero_edges(xpad)
    for plane in range(1, planes + 1):
        build(st_ct, ctpad, plane, -1)
    wait_halo(ctpad, everything, sct, rct, 0)
    build(st_ct, ctpad, 0, -1)
    build(st_ct, ctpad, planes + 1, -1)

    def reverse_parts(weight_t, stack, sums, outgoing, incoming, ssem, rsem):
        def keep(d, cols, total):
            sums[d, :, cols] = total

        convolve(weight_t, stack, keep, reverse=True)
        for k in range(1, nc):
            target = lax.rem(ci + k, nc)
            outgoing[k - 1] = sums[:, rows_of(target), :].astype(outgoing.dtype)
            send(outgoing.at[k - 1], incoming.at[k - 1], ssem.at[k - 1], rsem.at[k - 1], "chan", target).start()

    def part_copies(outgoing, incoming, ssem, rsem):
        return [send(outgoing.at[k - 1], incoming.at[k - 1], ssem.at[k - 1], rsem.at[k - 1],
                     "chan", lax.rem(ci + k, nc)) for k in range(1, nc)]

    reverse_parts(w2t_ref, st_ct, gh, part_out, part_in, sgh, rgh)

    gather_and_forward(xpad, sx, rx, sxh, rxh)
    for plane in range(1, planes + 1):
        build(wide, xpad, plane)
    for k in range(nc):
        wait_halo(xpad, rows_of(lax.rem(ci + nc - k, nc)), sxh, rxh, k)
    build(wide, xpad, 0)
    build(wide, xpad, planes + 1)

    def hidden_out(d, cols, total):
        pre[d, :, cols] = total
        hpad[d + 1, own, cols] = (total * jax.nn.sigmoid(total)).astype(BF16)

    convolve(w1_ref, wide, hidden_out)
    for copy in gather_sends(hpad, sh, rh):
        copy.start()
    start_halo(hpad, own, shh, rhh, 0)
    zero_edges(hpad)
    zero_edges(gppad)

    for copy in part_copies(part_out, part_in, sgh, rgh):
        copy.wait_recv()

    def slope(step, _):
        d = step // (n // 16)
        rows = pl.ds(pl.multiple_of((step % (n // 16)) * 16, 16), 16)
        total = gh[d, pl.ds(pl.multiple_of(ci * n + (step % (n // 16)) * 16, 16), 16), :]
        for k in range(nc - 1):
            total = total + part_in[k, d, rows, :].astype(F32)
        values = pre[d, rows, :]
        sigma = jax.nn.sigmoid(values)
        gppad[d + 1, rows, :] = (total * (sigma * (1.0 + values * (1.0 - sigma)))).astype(BF16)
        return 0

    lax.fori_loop(0, planes * (n // 16), slope, 0)
    start_halo(gppad, everything, sgp, rgp, 0)
    for plane in range(1, planes + 1):
        build(st_gp, gppad, plane, -1)
    filter_grad(g1, st_gp, xpad)

    nx = ns // 2
    core, xi = lax.rem(si, 2), si // 2
    half = nx * shard

    def span(core_index, x_index=None, samp_index=None):
        begin = core_index * half
        if x_index is None:
            return pl.ds(pl.multiple_of(begin, 16), half)
        begin = begin + x_index * shard
        if samp_index is None:
            return pl.ds(pl.multiple_of(begin, 16), shard)
        return pl.ds(pl.multiple_of(begin + samp_index * piece, 16), piece)

    class Reduction:
        def __init__(self, which, total, buffers, result):
            self.total, self.result = total, result
            self.out1, self.in1, self.out2, self.in2, self.out3, self.in3 = buffers
            self.base = which * 2 * (1 + ns + nz)

        def over_core(self, src, dst, at):
            return send(src, dst, sred.at[self.base + at], rred.at[self.base + at], "slab", 2 * xi + 1 - core)

        def over_x(self, src, dst, k, at):
            return send(src, dst, sred.at[self.base + at], rred.at[self.base + at], "slab",
                        2 * lax.rem(xi + k, nx) + core)

        def over_samp(self, src, dst, k, at):
            return send(src, dst, sred.at[self.base + at], rred.at[self.base + at], "samp", lax.rem(zi + k, nz))

        def core_sum(self):
            return [self.over_core(self.out1, self.in1, 0)]

        def x_sum(self):
            return [self.over_x(self.out2.at[k - 1], self.in2.at[k - 1], k, 1 + k) for k in range(1, nx)]

        def samp_sum(self):
            return [self.over_samp(self.out3.at[k - 1], self.in3.at[k - 1], k, 1 + nx + k) for k in range(1, nz)]

        def samp_gather(self, arriving):
            out = []
            for k in range(1, nz):
                rows = span(core, xi, lax.rem(zi + nz - k, nz) if arriving else zi)
                out.append(self.over_samp(self.result.at[rows], self.result.at[rows], k, 1 + nx + nz + k))
            return out

        def x_gather(self, arriving):
            out = []
            for k in range(1, nx):
                rows = span(core, lax.rem(xi + nx - k, nx) if arriving else xi)
                out.append(self.over_x(self.result.at[rows], self.result.at[rows], k, 1 + nx + 2 * nz + k))
            return out

        def core_gather(self, arriving):
            rows = span(1 - core if arriving else core)
            return [self.over_core(self.result.at[rows], self.result.at[rows], 1)]

        def one(self):
            self.out1[...] = self.total[span(1 - core), :].astype(self.out1.dtype)
            self.core_sum()[0].start()

        def two(self):
            self.core_sum()[0].wait_recv()
            copies = self.x_sum()
            for k in range(nx):
                x_index = lax.rem(xi + k, nx)
                local = pl.ds(pl.multiple_of(x_index * shard, 16), shard)
                summed = self.total[span(core, x_index), :] + self.in1[local, :].astype(F32)
                if k:
                    self.out2[k - 1] = summed.astype(self.out2.dtype)
                    copies[k - 1].start()
                else:
                    self.total[span(core, xi), :] = summed

        def three(self):
            for copy in self.x_sum():
                copy.wait_recv()
            copies = self.samp_sum()
            for k in range(nz):
                samp_index = lax.rem(zi + k, nz)
                rows = span(core, xi, samp_index)
                summed = self.total[rows, :]
                for m in range(nx - 1):
                    summed = summed + self.in2[m, pl.ds(pl.multiple_of(samp_index * piece, 16), piece), :].astype(F32)
                if k:
                    self.out3[k - 1] = summed.astype(self.out3.dtype)
                    copies[k - 1].start()
                else:
                    self.total[rows, :] = summed

        def four(self):
            for copy in self.samp_sum():
                copy.wait_recv()
            rows = span(core, xi, zi)
            summed = self.total[rows, :]
            for k in range(nz - 1):
                summed = summed + self.in3[k].astype(F32)
            self.result[rows, :] = (summed * norm_scale).astype(BF16)
            for copy in self.samp_gather(False):
                copy.start()

        def five(self):
            for copy in self.samp_gather(True):
                copy.wait_recv()
            for copy in self.x_gather(False):
                copy.start()

        def six(self):
            for copy in self.x_gather(True):
                copy.wait_recv()
            self.core_gather(False)[0].start()

        def seven(self):
            self.core_gather(True)[0].wait_recv()

        def finish(self):
            for copy in (self.core_sum() + self.x_sum() + self.samp_sum() + self.samp_gather(False)
                         + self.x_gather(False) + self.core_gather(False)):
                copy.wait_send()

    first = Reduction(0, g1, sums1, q1_ref)
    second = Reduction(1, g2, sums2, q2_ref)
    first.one()

    wait_halo(gppad, everything, sgp, rgp, 0)
    build(st_gp, gppad, 0, -1)
    build(st_gp, gppad, planes + 1, -1)
    reverse_parts(w1t_ref, st_gp, back, back_out, back_in, sbk, rbk)

    first.two()
    gather_and_forward(hpad, sh, rh, shh, rhh)
    for k in range(nc):
        wait_halo(hpad, rows_of(lax.rem(ci + nc - k, nc)), shh, rhh, k)
    filter_grad(g2, st_ct, hpad)
    second.one()
    first.three()
    for plane in range(planes):
        build(wide, hpad, plane)
    second.two()
    for plane in range(planes, planes + 2):
        build(wide, hpad, plane)

    def block(d, cols, total):
        out_ref[d, :, cols] = (x_ref[d, :, cols].astype(F32) + total).astype(BF16)

    first.four()
    convolve(w2_ref, wide, block)
    second.three()
    first.five()

    for copy in part_copies(back_out, back_in, sbk, rbk):
        copy.wait_recv()

    def volume_grad(step, _):
        d = step // (n // 16)
        rows = pl.ds(pl.multiple_of((step % (n // 16)) * 16, 16), 16)
        total = back[d, pl.ds(pl.multiple_of(ci * n + (step % (n // 16)) * 16, 16), 16), :]
        for k in range(nc - 1):
            total = total + back_in[k, d, rows, :].astype(F32)
        gv_ref[d, rows, :] = (ct_ref[d, rows, :].astype(F32) + total).astype(BF16)
        return 0

    lax.fori_loop(0, planes * (n // 16), volume_grad, 0)
    second.four()
    first.six()
    second.five()
    second.six()
    first.seven()
    second.seven()

    for copy in gather_sends(xpad, sx, rx) + gather_sends(hpad, sh, rh):
        copy.wait_send()
    for copy in part_copies(part_out, part_in, sgh, rgh) + part_copies(back_out, back_in, sbk, rbk):
        copy.wait_send()
    for k in range(nc):
        rows = rows_of(lax.rem(ci + nc - k, nc))
        finish_halo(xpad, rows, sxh, rxh, k)
        finish_halo(hpad, rows, shh, rhh, k)
    finish_halo(ctpad, everything, sct, rct, 0)
    finish_halo(gppad, everything, sgp, rgp, 0)
    first.finish()
    second.finish()


def per_device(volume, cotangent, filter_one, filter_two):
    n, planes, cells = volume.shape[1:]
    nz, ns, nc = (lax.axis_size(axis) for axis in ("samp", "slab", "chan"))
    channels = n * nc
    norm_scale = 1.0 / math.sqrt(nz * planes * ns * cells)
    unit = 16 * ns * nz
    rows = -(-27 * n // unit) * unit
    shard, piece = rows // ns, rows // ns // nz

    def forward(weight):
        return jnp.transpose(weight.reshape(n, 3, 9 * channels), (1, 0, 2))

    def backward(weight):
        return jnp.transpose(weight.reshape(n, 3, 9, channels), (1, 3, 2, 0)).reshape(3, channels, 9 * n)

    x = jnp.transpose(volume[0], (1, 0, 2))
    ct = jnp.transpose(cotangent[0], (1, 0, 2))
    vmem = pl.BlockSpec(memory_space=pltpu.VMEM)
    padded = planes + 2
    dma = pltpu.SemaphoreType.DMA

    nx = ns // 2

    def reduction_buffers(dtypes):
        one, two, three = dtypes
        return [pltpu.VMEM((nx * shard, channels), one)] * 2 + [
            pltpu.VMEM((nx - 1, shard, channels), two)] * 2 + [
            pltpu.VMEM((nz - 1, piece, channels), three)] * 2

    scratch = [
        pltpu.VMEM((padded, channels, cells), BF16),
        pltpu.VMEM((padded, channels, cells), BF16),
        pltpu.VMEM((padded, n, cells), BF16),
        pltpu.VMEM((padded, n, cells), BF16),
        pltpu.VMEM((padded, 9 * channels, cells), BF16),
        pltpu.VMEM((padded, 9 * n, cells), BF16),
        pltpu.VMEM((padded, 9 * n, cells), BF16),
        pltpu.VMEM((planes, n, cells), F32),
        pltpu.VMEM((planes, channels, cells), F32),
        pltpu.VMEM((planes, channels, cells), F32),
    ] + [pltpu.VMEM((nc - 1, planes, n, cells), BF16)] * 4 + [
        pltpu.VMEM((rows, channels), F32),
        pltpu.VMEM((rows, channels), F32),
        reduction_buffers(SUM_TYPES[0]),
        reduction_buffers(SUM_TYPES[1]),
        dma((planes * nc,)), dma((planes * nc,)), dma((2 * nc,)), dma((2 * nc,)),
        dma((2,)), dma((2,)), dma((nc,)), dma((nc,)),
        dma((planes * nc,)), dma((planes * nc,)), dma((2 * nc,)), dma((2 * nc,)),
        dma((2,)), dma((2,)), dma((nc,)), dma((nc,)),
        dma((4 * (1 + ns + nz),)), dma((4 * (1 + ns + nz),)),
    ]
    sizes = (nz, ns, nc, n, planes, shard, piece, norm_scale)
    block, grad_volume, one, two = pl.pallas_call(
        functools.partial(kernel, sizes),
        out_shape=(
            jax.ShapeDtypeStruct((planes, n, cells), BF16),
            jax.ShapeDtypeStruct((planes, n, cells), BF16),
            jax.ShapeDtypeStruct((rows, channels), BF16),
            jax.ShapeDtypeStruct((rows, channels), BF16),
        ),
        in_specs=[vmem] * 6,
        out_specs=(vmem,) * 4,
        scratch_shapes=scratch,
        compiler_params=pltpu.CompilerParams(
            collective_id=0, has_side_effects=True, vmem_limit_bytes=56 * 1024 * 1024),
        cost_estimate=pl.CostEstimate(
            flops=6 * 2 * planes * cells * n * 27 * channels, bytes_accessed=8 << 20, transcendentals=planes * n * cells),
        name="residual_pair",
    )(x, ct, forward(filter_one), forward(filter_two), backward(filter_one), backward(filter_two))

    def filter_out(values):
        values = values[: 27 * n].reshape(3, 9, n, channels)
        return jnp.transpose(values, (2, 0, 1, 3)).reshape(n, 27, channels).astype(F32)

    return (
        jnp.transpose(block, (1, 0, 2))[None],
        jnp.transpose(grad_volume, (1, 0, 2))[None],
        filter_out(one),
        filter_out(two),
    )


def solution(mesh):
    return jax.shard_map(
        per_device,
        mesh=mesh,
        in_specs=(
            P("samp", "chan", "slab", None),
            P("samp", "chan", "slab", None),
            P("chan", None, None),
            P("chan", None, None),
        ),
        out_specs=(
            P("samp", "chan", "slab", None),
            P("samp", "chan", "slab", None),
            P("chan", None, None),
            P("chan", None, None),
        ),
        check_vma=False,
    )
```

```python
import functools
import math

import jax
import jax.numpy as jnp
from jax import lax
from jax.experimental import pallas as pl
from jax.experimental.pallas import tpu as pltpu
from jax.sharding import PartitionSpec as P

SIDE = 32
CELLS = SIDE * SIDE
LANES = 128
GROUPS = LANES // SIDE
BLOCKS = CELLS // LANES
TILE = 256
MESH = pl.DeviceIdType.MESH
F32 = jnp.float32
BF16 = jnp.bfloat16

plane_offsets = [(-1, -1), (-1, 0), (-1, 1), (0, -1), (0, 0), (0, 1), (1, -1), (1, 0), (1, 1)]
SUM_TYPES = ((F32, F32, F32), (BF16, BF16, BF16))


def kernel(sizes, x_ref, ct_ref, w1_ref, w2_ref,
           out_ref, gv_ref, q1_ref, q2_ref,
           fw1, fw2, bw1, bw2, result, xpad, hpad, ctpad, gppad, wide, st_ct, st_gp, pre, gh, back,
           part_out, part_in, back_out, back_in,
           g1, g2, sums1, sums2,
           sx, rx, sxh, rxh, sct, rct, sgh, rgh, sh, rh, shh, rhh, sgp, rgp, sbk, rbk, sred, rred):
    nz, ns, nc, n, planes, shard, piece, norm_scale = sizes
    channels = n * nc
    zi, si, ci = lax.axis_index("samp"), lax.axis_index("slab"), lax.axis_index("chan")
    has_low, has_high = si > 0, si < ns - 1

    barrier = pltpu.get_barrier_semaphore()
    for k in range(1, nc):
        pl.semaphore_signal(barrier, inc=1, device_id={"chan": lax.rem(ci + k, nc)}, device_id_type=MESH)
    for k in range(1, ns):
        pl.semaphore_signal(barrier, inc=1, device_id={"slab": lax.rem(si + k, ns)}, device_id_type=MESH)
    for k in range(1, nz):
        pl.semaphore_signal(barrier, inc=1, device_id={"samp": lax.rem(zi + k, nz)}, device_id_type=MESH)
    pl.semaphore_wait(barrier, nc + ns + nz - 3)

    def rows_of(index):
        return pl.ds(pl.multiple_of(index * n, n), n)

    def send(src, dst, send_sem, recv_sem, axis, index):
        return pltpu.make_async_remote_copy(
            src_ref=src, dst_ref=dst, send_sem=send_sem, recv_sem=recv_sem,
            device_id={axis: index}, device_id_type=MESH)

    def halo_sends(padded, rows, ssem, rsem, slot):
        low = send(padded.at[1, rows], padded.at[planes + 1, rows], ssem.at[2 * slot], rsem.at[2 * slot], "slab", si - 1)
        high = send(padded.at[planes, rows], padded.at[0, rows], ssem.at[2 * slot + 1], rsem.at[2 * slot + 1], "slab", si + 1)
        return low, high

    def start_halo(*args):
        low, high = halo_sends(*args)
        pl.when(has_low)(low.start)
        pl.when(has_high)(high.start)

    def wait_halo(*args):
        low, high = halo_sends(*args)
        pl.when(has_high)(low.wait_recv)
        pl.when(has_low)(high.wait_recv)

    def finish_halo(*args):
        low, high = halo_sends(*args)
        pl.when(has_low)(low.wait_send)
        pl.when(has_high)(high.wait_send)

    own = rows_of(ci)
    everything = pl.ds(0, n)
    inside = pl.ds(1, planes)

    def gather_sends(padded, ssem, rsem):
        return [send(padded.at[1 + d, own], padded.at[1 + d, own], ssem.at[planes * (k - 1) + d],
                     rsem.at[planes * (k - 1) + d], "chan", lax.rem(ci + k, nc))
                for d in range(planes) for k in range(1, nc)]

    def gather_and_forward(padded, ssem, rsem, fsend, frecv):
        for d in range(planes):
            for k in range(1, nc):
                rows = rows_of(lax.rem(ci + nc - k, nc))
                at = planes * (k - 1) + d
                send(padded.at[1 + d, rows], padded.at[1 + d, rows], ssem.at[at], rsem.at[at],
                     "chan", lax.rem(ci + k, nc)).wait_recv()
                low, high = halo_sends(padded, rows, fsend, frecv, k)
                if d == 0:
                    pl.when(has_low)(low.start)
                if d == planes - 1:
                    pl.when(has_high)(high.start)

    def zero_edges(padded):
        @pl.when(jnp.logical_not(has_low))
        def _():
            padded[0] = jnp.zeros(padded.shape[1:], BF16)

        @pl.when(jnp.logical_not(has_high))
        def _():
            padded[planes + 1] = jnp.zeros(padded.shape[1:], BF16)

    lane = lax.broadcasted_iota(jnp.int32, (1, LANES), 1)
    group, column = lane // SIDE, lane % SIDE

    def mask_of(ok):
        return jnp.where(ok, 1.0, 0.0).astype(BF16)

    def kept(group_step, c):
        return mask_of((group + group_step >= 0) & (group + group_step < GROUPS)
                       & (column + c >= 0) & (column + c < SIDE))

    group_masks = [mask_of(group == g) for g in range(GROUPS)]
    shift_masks = {(step, c): kept(step, c) for step in (-1, 0, 1) for c in (-1, 0, 1)}

    def lane_block(values, t):
        return values[:, t * LANES : (t + 1) * LANES]

    def turned(values, shift):
        return values if shift % LANES == 0 else pltpu.roll(values, shift % LANES, 1)

    def to_blocks(values):
        out = []
        for t in range(BLOCKS):
            total = None
            for g in range(GROUPS):
                row = BLOCKS * g + t
                term = turned(lane_block(values, row // GROUPS), SIDE * (g - row % GROUPS)) * group_masks[g]
                total = term if total is None else total + term
            out.append(total)
        return jnp.concatenate(out, axis=1)

    def from_blocks(values):
        out = []
        for m in range(BLOCKS):
            total = None
            for g in range(GROUPS):
                row = GROUPS * m + g
                term = turned(lane_block(values, row % BLOCKS), SIDE * (g - row // BLOCKS)) * group_masks[g]
                total = term if total is None else total + term
            out.append(total)
        return jnp.concatenate(out, axis=1)

    def build(stack, padded, plane, sign=1):
        count = padded.shape[1]
        height = min(32, count)

        def body(step, _):
            values = padded[plane, pl.ds(pl.multiple_of(step * height, 16), height), :]
            sources = [lane_block(values, t) for t in range(BLOCKS)]
            moved = {}
            for c in (-1, 0, 1):
                for t in range(BLOCKS):
                    moved[t, 0, c] = turned(sources[t], -c) * shift_masks[0, c] if c else sources[t]
                moved[0, 1, c] = turned(sources[0], -SIDE - c) * shift_masks[1, c]
                moved[BLOCKS - 1, -1, c] = turned(sources[BLOCKS - 1], SIDE - c) * shift_masks[-1, c]
            for j, (b, c) in enumerate(plane_offsets):
                b, c = sign * b, sign * c
                for t in range(BLOCKS):
                    source = t + b
                    wrap = 1 if source == BLOCKS else -1 if source < 0 else 0
                    stack[plane, pl.ds(pl.multiple_of(j * count + step * height, 16), height),
                          t * LANES : (t + 1) * LANES] = moved[source % BLOCKS, wrap, c]
            return 0

        lax.fori_loop(0, count // height, body, 0)

    def lay_forward(target, weight):
        for tap in range(27):
            target[tap // 9, :, (tap % 9) * channels : (tap % 9 + 1) * channels] = weight[tap]

    def lay_backward(target, weight):
        group_size = max(1, LANES // n)
        for a in range(3):
            for j in range(0, 9, group_size):
                taps = min(group_size, 9 - j)
                piece_of = weight[pl.ds(9 * a + j, taps)].reshape(taps * n, channels)
                target[a, :, j * n : (j + taps) * n] = piece_of.T

    def convolve(weight, stack, emit, reverse=False):
        def body(step, _):
            cols = pl.ds(pl.multiple_of(step * TILE, TILE), TILE)
            totals = [None] * planes
            for p in range(planes + 2):
                pairs = []
                for d in range(planes):
                    a = d + 2 - p if reverse else p - d
                    if 0 <= a < 3:
                        pairs.append((d, a))
                left = jnp.concatenate([weight[a] for _, a in pairs], axis=0)
                term = jnp.dot(left, stack[p, :, cols], preferred_element_type=F32)
                height = weight.shape[1]
                for at, (d, _) in enumerate(pairs):
                    part = term[at * height : (at + 1) * height]
                    totals[d] = part if totals[d] is None else totals[d] + part
            for d in range(planes):
                emit(d, cols, totals[d])
            return 0

        lax.fori_loop(0, CELLS // TILE, body, 0)

    def filter_grad(total_ref, stack, padded):
        count = stack.shape[1]
        for a in range(3):
            total = None
            for d in range(planes):
                term = lax.dot_general(stack[d + 1], padded[d + a], (((1,), (1,)), ((), ())),
                                       preferred_element_type=F32)
                total = term if total is None else total + term
            total_ref[pl.ds(a * count, count), :] = total
        rest = ns * shard - 3 * count
        if rest:
            total_ref[pl.ds(3 * count, rest), :] = jnp.zeros((rest, channels), F32)

    for d in range(planes):
        xpad[1 + d, own, :] = to_blocks(x_ref[d])
    for copy in gather_sends(xpad, sx, rx):
        copy.start()
    start_halo(xpad, own, sxh, rxh, 0)
    for d in range(planes):
        ctpad[1 + d] = to_blocks(ct_ref[d])
    start_halo(ctpad, everything, sct, rct, 0)

    lay_backward(bw2, w2_ref)
    zero_edges(ctpad)
    zero_edges(xpad)
    for plane in range(1, planes + 1):
        build(st_ct, ctpad, plane, -1)
    wait_halo(ctpad, everything, sct, rct, 0)
    build(st_ct, ctpad, 0, -1)
    build(st_ct, ctpad, planes + 1, -1)

    def reverse_parts(weight_t, stack, sums, outgoing, incoming, ssem, rsem):
        def keep(d, cols, total):
            sums[d, :, cols] = total

        convolve(weight_t, stack, keep, reverse=True)
        for k in range(1, nc):
            target = lax.rem(ci + k, nc)
            outgoing[k - 1] = sums[:, rows_of(target), :].astype(outgoing.dtype)
            send(outgoing.at[k - 1], incoming.at[k - 1], ssem.at[k - 1], rsem.at[k - 1], "chan", target).start()

    def part_copies(outgoing, incoming, ssem, rsem):
        return [send(outgoing.at[k - 1], incoming.at[k - 1], ssem.at[k - 1], rsem.at[k - 1],
                     "chan", lax.rem(ci + k, nc)) for k in range(1, nc)]

    reverse_parts(bw2, st_ct, gh, part_out, part_in, sgh, rgh)

    lay_forward(fw1, w1_ref)
    gather_and_forward(xpad, sx, rx, sxh, rxh)
    for plane in range(1, planes + 1):
        build(wide, xpad, plane)
    for k in range(nc):
        wait_halo(xpad, rows_of(lax.rem(ci + nc - k, nc)), sxh, rxh, k)
    build(wide, xpad, 0)
    build(wide, xpad, planes + 1)

    def hidden_out(d, cols, total):
        pre[d, :, cols] = total
        hpad[d + 1, own, cols] = (total * jax.nn.sigmoid(total)).astype(BF16)

    convolve(fw1, wide, hidden_out)
    for copy in gather_sends(hpad, sh, rh):
        copy.start()
    start_halo(hpad, own, shh, rhh, 0)
    zero_edges(hpad)
    lay_backward(bw1, w1_ref)
    lay_forward(fw2, w2_ref)
    zero_edges(gppad)

    for copy in part_copies(part_out, part_in, sgh, rgh):
        copy.wait_recv()

    def slope(step, _):
        d = step // (n // 16)
        rows = pl.ds(pl.multiple_of((step % (n // 16)) * 16, 16), 16)
        total = gh[d, pl.ds(pl.multiple_of(ci * n + (step % (n // 16)) * 16, 16), 16), :]
        for k in range(nc - 1):
            total = total + part_in[k, d, rows, :].astype(F32)
        values = pre[d, rows, :]
        sigma = jax.nn.sigmoid(values)
        gppad[d + 1, rows, :] = (total * (sigma * (1.0 + values * (1.0 - sigma)))).astype(BF16)
        return 0

    lax.fori_loop(0, planes * (n // 16), slope, 0)
    start_halo(gppad, everything, sgp, rgp, 0)
    for plane in range(1, planes + 1):
        build(st_gp, gppad, plane, -1)
    filter_grad(g1, st_gp, xpad)

    nx = ns // 2
    core, xi = lax.rem(si, 2), si // 2
    half = nx * shard

    def span(core_index, x_index=None, samp_index=None):
        begin = core_index * half
        if x_index is None:
            return pl.ds(pl.multiple_of(begin, 16), half)
        begin = begin + x_index * shard
        if samp_index is None:
            return pl.ds(pl.multiple_of(begin, 16), shard)
        return pl.ds(pl.multiple_of(begin + samp_index * piece, 16), piece)

    class Reduction:
        def __init__(self, which, total, buffers, result):
            self.total, self.result = total, result
            self.out1, self.in1, self.out2, self.in2, self.out3, self.in3 = buffers
            self.base = which * 2 * (1 + ns + nz)

        def over_core(self, src, dst, at):
            return send(src, dst, sred.at[self.base + at], rred.at[self.base + at], "slab", 2 * xi + 1 - core)

        def over_x(self, src, dst, k, at):
            return send(src, dst, sred.at[self.base + at], rred.at[self.base + at], "slab",
                        2 * lax.rem(xi + k, nx) + core)

        def over_samp(self, src, dst, k, at):
            return send(src, dst, sred.at[self.base + at], rred.at[self.base + at], "samp", lax.rem(zi + k, nz))

        def core_sum(self):
            return [self.over_core(self.out1, self.in1, 0)]

        def x_sum(self):
            return [self.over_x(self.out2.at[k - 1], self.in2.at[k - 1], k, 1 + k) for k in range(1, nx)]

        def samp_sum(self):
            return [self.over_samp(self.out3.at[k - 1], self.in3.at[k - 1], k, 1 + nx + k) for k in range(1, nz)]

        def samp_gather(self, arriving):
            out = []
            for k in range(1, nz):
                rows = span(core, xi, lax.rem(zi + nz - k, nz) if arriving else zi)
                out.append(self.over_samp(self.result.at[rows], self.result.at[rows], k, 1 + nx + nz + k))
            return out

        def x_gather(self, arriving):
            out = []
            for k in range(1, nx):
                rows = span(core, lax.rem(xi + nx - k, nx) if arriving else xi)
                out.append(self.over_x(self.result.at[rows], self.result.at[rows], k, 1 + nx + 2 * nz + k))
            return out

        def core_gather(self, arriving):
            rows = span(1 - core if arriving else core)
            return [self.over_core(self.result.at[rows], self.result.at[rows], 1)]

        def one(self):
            self.out1[...] = self.total[span(1 - core), :].astype(self.out1.dtype)
            self.core_sum()[0].start()

        def two(self):
            self.core_sum()[0].wait_recv()
            copies = self.x_sum()
            for k in range(nx):
                x_index = lax.rem(xi + k, nx)
                local = pl.ds(pl.multiple_of(x_index * shard, 16), shard)
                summed = self.total[span(core, x_index), :] + self.in1[local, :].astype(F32)
                if k:
                    self.out2[k - 1] = summed.astype(self.out2.dtype)
                    copies[k - 1].start()
                else:
                    self.total[span(core, xi), :] = summed

        def three(self):
            for copy in self.x_sum():
                copy.wait_recv()
            copies = self.samp_sum()
            for k in range(nz):
                samp_index = lax.rem(zi + k, nz)
                rows = span(core, xi, samp_index)
                summed = self.total[rows, :]
                for m in range(nx - 1):
                    summed = summed + self.in2[m, pl.ds(pl.multiple_of(samp_index * piece, 16), piece), :].astype(F32)
                if k:
                    self.out3[k - 1] = summed.astype(self.out3.dtype)
                    copies[k - 1].start()
                else:
                    self.total[rows, :] = summed

        def four(self):
            for copy in self.samp_sum():
                copy.wait_recv()
            rows = span(core, xi, zi)
            summed = self.total[rows, :]
            for k in range(nz - 1):
                summed = summed + self.in3[k].astype(F32)
            self.result[rows, :] = (summed * norm_scale).astype(BF16)
            for copy in self.samp_gather(False):
                copy.start()

        def five(self):
            for copy in self.samp_gather(True):
                copy.wait_recv()
            for copy in self.x_gather(False):
                copy.start()

        def six(self):
            for copy in self.x_gather(True):
                copy.wait_recv()
            self.core_gather(False)[0].start()

        def seven(self):
            self.core_gather(True)[0].wait_recv()

        def finish(self):
            for copy in (self.core_sum() + self.x_sum() + self.samp_sum() + self.samp_gather(False)
                         + self.x_gather(False) + self.core_gather(False)):
                copy.wait_send()

    first = Reduction(0, g1, sums1, q1_ref)
    second = Reduction(1, g2, sums2, q2_ref)
    first.one()

    wait_halo(gppad, everything, sgp, rgp, 0)
    build(st_gp, gppad, 0, -1)
    build(st_gp, gppad, planes + 1, -1)
    reverse_parts(bw1, st_gp, back, back_out, back_in, sbk, rbk)

    first.two()
    gather_and_forward(hpad, sh, rh, shh, rhh)
    for k in range(nc):
        wait_halo(hpad, rows_of(lax.rem(ci + nc - k, nc)), shh, rhh, k)
    filter_grad(g2, st_ct, hpad)
    second.one()
    first.three()
    for plane in range(planes):
        build(wide, hpad, plane)
    second.two()
    for plane in range(planes, planes + 2):
        build(wide, hpad, plane)

    def block(d, cols, total):
        result[d, :, cols] = (xpad[1 + d, own, cols].astype(F32) + total).astype(BF16)

    first.four()
    convolve(fw2, wide, block)
    second.three()
    first.five()
    for d in range(planes):
        out_ref[d] = from_blocks(result[d])

    for copy in part_copies(back_out, back_in, sbk, rbk):
        copy.wait_recv()

    def volume_grad(step, _):
        d = step // (n // 16)
        rows = pl.ds(pl.multiple_of((step % (n // 16)) * 16, 16), 16)
        total = back[d, pl.ds(pl.multiple_of(ci * n + (step % (n // 16)) * 16, 16), 16), :]
        for k in range(nc - 1):
            total = total + back_in[k, d, rows, :].astype(F32)
        gv_ref[d, rows, :] = from_blocks((ctpad[d + 1, rows, :].astype(F32) + total).astype(BF16))
        return 0

    lax.fori_loop(0, planes * (n // 16), volume_grad, 0)
    second.four()
    first.six()
    second.five()
    second.six()
    first.seven()
    second.seven()

    for copy in gather_sends(xpad, sx, rx) + gather_sends(hpad, sh, rh):
        copy.wait_send()
    for copy in part_copies(part_out, part_in, sgh, rgh) + part_copies(back_out, back_in, sbk, rbk):
        copy.wait_send()
    for k in range(nc):
        rows = rows_of(lax.rem(ci + nc - k, nc))
        finish_halo(xpad, rows, sxh, rxh, k)
        finish_halo(hpad, rows, shh, rhh, k)
    finish_halo(ctpad, everything, sct, rct, 0)
    finish_halo(gppad, everything, sgp, rgp, 0)
    first.finish()
    second.finish()


def per_device(volume, cotangent, filter_one, filter_two):
    n, planes, cells = volume.shape[1:]
    nz, ns, nc = (lax.axis_size(axis) for axis in ("samp", "slab", "chan"))
    channels = n * nc
    norm_scale = 1.0 / math.sqrt(nz * planes * ns * cells)
    unit = 16 * ns * nz
    rows = -(-27 * n // unit) * unit
    shard, piece = rows // ns, rows // ns // nz

    def by_tap(weight):
        return jnp.transpose(weight, (1, 0, 2))

    x = jnp.transpose(volume[0], (1, 0, 2))
    ct = jnp.transpose(cotangent[0], (1, 0, 2))
    vmem = pl.BlockSpec(memory_space=pltpu.VMEM)
    padded = planes + 2
    dma = pltpu.SemaphoreType.DMA

    nx = ns // 2

    def reduction_buffers(dtypes):
        one, two, three = dtypes
        return [pltpu.VMEM((nx * shard, channels), one)] * 2 + [
            pltpu.VMEM((nx - 1, shard, channels), two)] * 2 + [
            pltpu.VMEM((nz - 1, piece, channels), three)] * 2

    scratch = [pltpu.VMEM((3, n, 9 * channels), BF16)] * 2 + [pltpu.VMEM((3, channels, 9 * n), BF16)] * 2 + [
        pltpu.VMEM((planes, n, cells), BF16),
        pltpu.VMEM((padded, channels, cells), BF16),
        pltpu.VMEM((padded, channels, cells), BF16),
        pltpu.VMEM((padded, n, cells), BF16),
        pltpu.VMEM((padded, n, cells), BF16),
        pltpu.VMEM((padded, 9 * channels, cells), BF16),
        pltpu.VMEM((padded, 9 * n, cells), BF16),
        pltpu.VMEM((padded, 9 * n, cells), BF16),
        pltpu.VMEM((planes, n, cells), F32),
        pltpu.VMEM((planes, channels, cells), F32),
        pltpu.VMEM((planes, channels, cells), F32),
    ] + [pltpu.VMEM((nc - 1, planes, n, cells), BF16)] * 4 + [
        pltpu.VMEM((rows, channels), F32),
        pltpu.VMEM((rows, channels), F32),
        reduction_buffers(SUM_TYPES[0]),
        reduction_buffers(SUM_TYPES[1]),
        dma((planes * nc,)), dma((planes * nc,)), dma((2 * nc,)), dma((2 * nc,)),
        dma((2,)), dma((2,)), dma((nc,)), dma((nc,)),
        dma((planes * nc,)), dma((planes * nc,)), dma((2 * nc,)), dma((2 * nc,)),
        dma((2,)), dma((2,)), dma((nc,)), dma((nc,)),
        dma((4 * (1 + ns + nz),)), dma((4 * (1 + ns + nz),)),
    ]
    sizes = (nz, ns, nc, n, planes, shard, piece, norm_scale)
    block, grad_volume, one, two = pl.pallas_call(
        functools.partial(kernel, sizes),
        out_shape=(
            jax.ShapeDtypeStruct((planes, n, cells), BF16),
            jax.ShapeDtypeStruct((planes, n, cells), BF16),
            jax.ShapeDtypeStruct((rows, channels), BF16),
            jax.ShapeDtypeStruct((rows, channels), BF16),
        ),
        in_specs=[vmem] * 4,
        out_specs=(vmem,) * 4,
        scratch_shapes=scratch,
        compiler_params=pltpu.CompilerParams(
            collective_id=0, has_side_effects=True, vmem_limit_bytes=56 * 1024 * 1024),
        cost_estimate=pl.CostEstimate(
            flops=6 * 2 * planes * cells * n * 27 * channels, bytes_accessed=8 << 20, transcendentals=planes * n * cells),
        name="residual_pair",
    )(x, ct, by_tap(filter_one), by_tap(filter_two))

    def filter_out(values):
        values = values[: 27 * n].reshape(3, 9, n, channels)
        return jnp.transpose(values, (2, 0, 1, 3)).reshape(n, 27, channels).astype(F32)

    return (
        jnp.transpose(block, (1, 0, 2))[None],
        jnp.transpose(grad_volume, (1, 0, 2))[None],
        filter_out(one),
        filter_out(two),
    )


def solution(mesh):
    return jax.shard_map(
        per_device,
        mesh=mesh,
        in_specs=(
            P("samp", "chan", "slab", None),
            P("samp", "chan", "slab", None),
            P("chan", None, None),
            P("chan", None, None),
        ),
        out_specs=(
            P("samp", "chan", "slab", None),
            P("samp", "chan", "slab", None),
            P("chan", None, None),
            P("chan", None, None),
        ),
        check_vma=False,
    )
```

```python
import functools
import math

import jax
import jax.numpy as jnp
from jax import lax
from jax.experimental import pallas as pl
from jax.experimental.pallas import tpu as pltpu
from jax.sharding import PartitionSpec as P

SIDE = 32
CELLS = SIDE * SIDE
LANES = 128
GROUPS = LANES // SIDE
BLOCKS = CELLS // LANES
TILE = 256
MESH = pl.DeviceIdType.MESH
F32 = jnp.float32
BF16 = jnp.bfloat16

plane_offsets = [(-1, -1), (-1, 0), (-1, 1), (0, -1), (0, 0), (0, 1), (1, -1), (1, 0), (1, 1)]
SUM_TYPES = ((BF16, BF16, BF16), (BF16, BF16, BF16))


def kernel(sizes, x_ref, ct_ref, w1_ref, w2_ref,
           out_ref, gv_ref, q1_ref, q2_ref,
           fw1, fw2, bw1, bw2, wall1, wall2, result, xpad, hpad, ctpad, gppad, wide, st_ct, st_gp, pre,
           g1, g2, sums1, sums2,
           sx, rx, sxh, rxh, sct, rct, scth, rcth, shh, rhh, sgp, rgp, sw, rw, sred, rred):
    nz, ns, nc, n, planes, shard, piece, norm_scale = sizes
    channels = n * nc
    zi, si, ci = lax.axis_index("samp"), lax.axis_index("slab"), lax.axis_index("chan")
    has_low, has_high = si > 0, si < ns - 1

    barrier = pltpu.get_barrier_semaphore()
    for k in range(1, nc):
        pl.semaphore_signal(barrier, inc=1, device_id={"chan": lax.rem(ci + k, nc)}, device_id_type=MESH)
    for k in range(1, ns):
        pl.semaphore_signal(barrier, inc=1, device_id={"slab": lax.rem(si + k, ns)}, device_id_type=MESH)
    for k in range(1, nz):
        pl.semaphore_signal(barrier, inc=1, device_id={"samp": lax.rem(zi + k, nz)}, device_id_type=MESH)
    pl.semaphore_wait(barrier, nc + ns + nz - 3)

    def rows_of(index):
        return pl.ds(pl.multiple_of(index * n, n), n)

    def send(src, dst, send_sem, recv_sem, axis, index):
        return pltpu.make_async_remote_copy(
            src_ref=src, dst_ref=dst, send_sem=send_sem, recv_sem=recv_sem,
            device_id={axis: index}, device_id_type=MESH)

    def halo_sends(padded, rows, ssem, rsem, slot):
        low = send(padded.at[1, rows], padded.at[planes + 1, rows], ssem.at[2 * slot], rsem.at[2 * slot], "slab", si - 1)
        high = send(padded.at[planes, rows], padded.at[0, rows], ssem.at[2 * slot + 1], rsem.at[2 * slot + 1], "slab", si + 1)
        return low, high

    def start_halo(*args):
        low, high = halo_sends(*args)
        pl.when(has_low)(low.start)
        pl.when(has_high)(high.start)

    def wait_halo(*args):
        low, high = halo_sends(*args)
        pl.when(has_high)(low.wait_recv)
        pl.when(has_low)(high.wait_recv)

    def finish_halo(*args):
        low, high = halo_sends(*args)
        pl.when(has_low)(low.wait_send)
        pl.when(has_high)(high.wait_send)

    own = rows_of(ci)
    everything = pl.ds(0, channels)
    inside = pl.ds(1, planes)

    def gather_sends(padded, ssem, rsem):
        return [send(padded.at[1 + d, own], padded.at[1 + d, own], ssem.at[planes * (k - 1) + d],
                     rsem.at[planes * (k - 1) + d], "chan", lax.rem(ci + k, nc))
                for d in range(planes) for k in range(1, nc)]

    def gather_and_forward(padded, ssem, rsem, fsend, frecv):
        for d in range(planes):
            for k in range(1, nc):
                rows = rows_of(lax.rem(ci + nc - k, nc))
                at = planes * (k - 1) + d
                send(padded.at[1 + d, rows], padded.at[1 + d, rows], ssem.at[at], rsem.at[at],
                     "chan", lax.rem(ci + k, nc)).wait_recv()
                low, high = halo_sends(padded, rows, fsend, frecv, k)
                if d == 0:
                    pl.when(has_low)(low.start)
                if d == planes - 1:
                    pl.when(has_high)(high.start)

    def zero_edges(padded):
        @pl.when(jnp.logical_not(has_low))
        def _():
            padded[0] = jnp.zeros(padded.shape[1:], BF16)

        @pl.when(jnp.logical_not(has_high))
        def _():
            padded[planes + 1] = jnp.zeros(padded.shape[1:], BF16)

    lane = lax.broadcasted_iota(jnp.int32, (1, LANES), 1)
    group, column = lane // SIDE, lane % SIDE

    def mask_of(ok):
        return jnp.where(ok, 1.0, 0.0).astype(BF16)

    def kept(group_step, c):
        return mask_of((group + group_step >= 0) & (group + group_step < GROUPS)
                       & (column + c >= 0) & (column + c < SIDE))

    group_masks = [mask_of(group == g) for g in range(GROUPS)]
    shift_masks = {(step, c): kept(step, c) for step in (-1, 0, 1) for c in (-1, 0, 1)}

    def lane_block(values, t):
        return values[:, t * LANES : (t + 1) * LANES]

    def turned(values, shift):
        return values if shift % LANES == 0 else pltpu.roll(values, shift % LANES, 1)

    def to_blocks(values):
        out = []
        for t in range(BLOCKS):
            total = None
            for g in range(GROUPS):
                row = BLOCKS * g + t
                term = turned(lane_block(values, row // GROUPS), SIDE * (g - row % GROUPS)) * group_masks[g]
                total = term if total is None else total + term
            out.append(total)
        return jnp.concatenate(out, axis=1)

    def from_blocks(values):
        out = []
        for m in range(BLOCKS):
            total = None
            for g in range(GROUPS):
                row = GROUPS * m + g
                term = turned(lane_block(values, row % BLOCKS), SIDE * (g - row // BLOCKS)) * group_masks[g]
                total = term if total is None else total + term
            out.append(total)
        return jnp.concatenate(out, axis=1)

    def build(stack, padded, plane, sign=1):
        count = padded.shape[1]
        height = min(32, count)

        def body(step, _):
            values = padded[plane, pl.ds(pl.multiple_of(step * height, 16), height), :]
            sources = [lane_block(values, t) for t in range(BLOCKS)]
            moved = {}
            for c in (-1, 0, 1):
                for t in range(BLOCKS):
                    moved[t, 0, c] = turned(sources[t], -c) * shift_masks[0, c] if c else sources[t]
                moved[0, 1, c] = turned(sources[0], -SIDE - c) * shift_masks[1, c]
                moved[BLOCKS - 1, -1, c] = turned(sources[BLOCKS - 1], SIDE - c) * shift_masks[-1, c]
            for j, (b, c) in enumerate(plane_offsets):
                b, c = sign * b, sign * c
                for t in range(BLOCKS):
                    source = t + b
                    wrap = 1 if source == BLOCKS else -1 if source < 0 else 0
                    stack[plane, pl.ds(pl.multiple_of(j * count + step * height, 16), height),
                          t * LANES : (t + 1) * LANES] = moved[source % BLOCKS, wrap, c]
            return 0

        lax.fori_loop(0, count // height, body, 0)

    def lay_forward(target, weight):
        for tap in range(27):
            target[tap // 9, :, (tap % 9) * channels : (tap % 9 + 1) * channels] = weight(tap)

    def lay_backward(target, weight):
        for tap in range(27):
            target[tap // 9, :, (tap % 9) * channels : (tap % 9 + 1) * channels] = weight(tap).T

    def all_outputs(wall):
        return lambda tap: jnp.concatenate([wall[q, tap * n : (tap + 1) * n, :] for q in range(nc)], axis=0)

    def convolve(weight, height, stack, emit, reverse=False):
        def body(step, _):
            cols = pl.ds(pl.multiple_of(step * TILE, TILE), TILE)
            totals = [None] * planes
            for p in range(planes + 2):
                pairs = []
                for d in range(planes):
                    a = d + 2 - p if reverse else p - d
                    if 0 <= a < 3:
                        pairs.append((d, a))
                left = jnp.concatenate([weight(a) for _, a in pairs], axis=0)
                term = jnp.dot(left, stack[p, :, cols], preferred_element_type=F32)
                for at, (d, _) in enumerate(pairs):
                    part = term[at * height : (at + 1) * height]
                    totals[d] = part if totals[d] is None else totals[d] + part
            for d in range(planes):
                emit(d, cols, totals[d])
            return 0

        lax.fori_loop(0, CELLS // TILE, body, 0)

    def filter_grad(total_ref, stack, padded):
        count = 9 * n
        for a in range(3):
            total = None
            for d in range(planes):
                left = jnp.concatenate(
                    [stack[d + 1, pl.ds(pl.multiple_of(j * channels + ci * n, n), n), :] for j in range(9)], axis=0)
                term = lax.dot_general(left, padded[d + a], (((1,), (1,)), ((), ())), preferred_element_type=F32)
                total = term if total is None else total + term
            total_ref[pl.ds(a * count, count), :] = total
        rest = ns * shard - 3 * count
        if rest:
            total_ref[pl.ds(3 * count, rest), :] = jnp.zeros((rest, channels), F32)

    nx = ns // 2
    core, xi = lax.rem(si, 2), si // 2
    half = nx * shard

    def span(core_index, x_index=None, samp_index=None):
        begin = core_index * half
        if x_index is None:
            return pl.ds(pl.multiple_of(begin, 16), half)
        begin = begin + x_index * shard
        if samp_index is None:
            return pl.ds(pl.multiple_of(begin, 16), shard)
        return pl.ds(pl.multiple_of(begin + samp_index * piece, 16), piece)

    class Reduction:
        def __init__(self, which, total, buffers, result):
            self.total, self.result = total, result
            self.out1, self.in1, self.out2, self.in2, self.out3, self.in3 = buffers
            self.base = which * 2 * (1 + ns + nz)

        def over_core(self, src, dst, at):
            return send(src, dst, sred.at[self.base + at], rred.at[self.base + at], "slab", 2 * xi + 1 - core)

        def over_x(self, src, dst, k, at):
            return send(src, dst, sred.at[self.base + at], rred.at[self.base + at], "slab",
                        2 * lax.rem(xi + k, nx) + core)

        def over_samp(self, src, dst, k, at):
            return send(src, dst, sred.at[self.base + at], rred.at[self.base + at], "samp", lax.rem(zi + k, nz))

        def core_sum(self):
            return [self.over_core(self.out1, self.in1, 0)]

        def x_sum(self):
            return [self.over_x(self.out2.at[k - 1], self.in2.at[k - 1], k, 1 + k) for k in range(1, nx)]

        def samp_sum(self):
            return [self.over_samp(self.out3.at[k - 1], self.in3.at[k - 1], k, 1 + nx + k) for k in range(1, nz)]

        def samp_gather(self, arriving):
            out = []
            for k in range(1, nz):
                rows = span(core, xi, lax.rem(zi + nz - k, nz) if arriving else zi)
                out.append(self.over_samp(self.result.at[rows], self.result.at[rows], k, 1 + nx + nz + k))
            return out

        def x_gather(self, arriving):
            out = []
            for k in range(1, nx):
                rows = span(core, lax.rem(xi + nx - k, nx) if arriving else xi)
                out.append(self.over_x(self.result.at[rows], self.result.at[rows], k, 1 + nx + 2 * nz + k))
            return out

        def core_gather(self, arriving):
            rows = span(1 - core if arriving else core)
            return [self.over_core(self.result.at[rows], self.result.at[rows], 1)]

        def one(self):
            self.out1[...] = self.total[span(1 - core), :].astype(self.out1.dtype)
            self.core_sum()[0].start()

        def two(self):
            self.core_sum()[0].wait_recv()
            copies = self.x_sum()
            for k in range(nx):
                x_index = lax.rem(xi + k, nx)
                local = pl.ds(pl.multiple_of(x_index * shard, 16), shard)
                summed = self.total[span(core, x_index), :] + self.in1[local, :].astype(F32)
                if k:
                    self.out2[k - 1] = summed.astype(self.out2.dtype)
                    copies[k - 1].start()
                else:
                    self.total[span(core, xi), :] = summed

        def three(self):
            for copy in self.x_sum():
                copy.wait_recv()
            copies = self.samp_sum()
            for k in range(nz):
                samp_index = lax.rem(zi + k, nz)
                rows = span(core, xi, samp_index)
                summed = self.total[rows, :]
                for m in range(nx - 1):
                    summed = summed + self.in2[m, pl.ds(pl.multiple_of(samp_index * piece, 16), piece), :].astype(F32)
                if k:
                    self.out3[k - 1] = summed.astype(self.out3.dtype)
                    copies[k - 1].start()
                else:
                    self.total[rows, :] = summed

        def four(self):
            for copy in self.samp_sum():
                copy.wait_recv()
            rows = span(core, xi, zi)
            summed = self.total[rows, :]
            for k in range(nz - 1):
                summed = summed + self.in3[k].astype(F32)
            self.result[rows, :] = (summed * norm_scale).astype(BF16)
            for copy in self.samp_gather(False):
                copy.start()

        def five(self):
            for copy in self.samp_gather(True):
                copy.wait_recv()
            for copy in self.x_gather(False):
                copy.start()

        def six(self):
            for copy in self.x_gather(True):
                copy.wait_recv()
            self.core_gather(False)[0].start()

        def seven(self):
            self.core_gather(True)[0].wait_recv()

        def finish(self):
            for copy in (self.core_sum() + self.x_sum() + self.samp_sum() + self.samp_gather(False)
                         + self.x_gather(False) + self.core_gather(False)):
                copy.wait_send()

    first = Reduction(0, g1, sums1, q1_ref)
    second = Reduction(1, g2, sums2, q2_ref)

    class Filter:
        def __init__(self, which, wall, k):
            self.wall, self.k = wall, k
            self.owner = lax.rem(ci + nc - k, nc)
            self.result = wall.at[self.owner]
            self.base = (which * nc + k) * (3 + ns + nz)

        def copy(self, rows, at, axis, index):
            ref = self.result.at[rows]
            return send(ref, ref, sw.at[self.base + at], rw.at[self.base + at], axis, index)

        def from_chan(self):
            rows = span(core, xi, zi)
            ref = self.wall.at[ci, rows]
            return send(ref, ref, sw.at[self.base], rw.at[self.base], "chan", lax.rem(ci + self.k, nc))

        def samp_gather(self, arriving):
            return [self.copy(span(core, xi, lax.rem(zi + nz - m, nz) if arriving else zi), 1 + m,
                              "samp", lax.rem(zi + m, nz)) for m in range(1, nz)]

        def x_gather(self, arriving):
            return [self.copy(span(core, lax.rem(xi + nx - m, nx) if arriving else xi), 1 + nz + m,
                              "slab", 2 * lax.rem(xi + m, nx) + core) for m in range(1, nx)]

        def core_gather(self, arriving):
            return [self.copy(span(1 - core if arriving else core), 1 + nz + nx, "slab", 2 * xi + 1 - core)]

        def zero(self):
            self.from_chan().start()

        def one(self):
            rows = span(core, xi, zi)
            ref = self.wall.at[self.owner, rows]
            send(ref, ref, sw.at[self.base], rw.at[self.base], "chan", lax.rem(ci + self.k, nc)).wait_recv()
            for copy in self.samp_gather(False):
                copy.start()

        def two(self):
            for copy in self.samp_gather(True):
                copy.wait_recv()
            for copy in self.x_gather(False):
                copy.start()

        def three(self):
            for copy in self.x_gather(True):
                copy.wait_recv()
            for copy in self.core_gather(False):
                copy.start()

        def four(self):
            for copy in self.core_gather(True):
                copy.wait_recv()

        def finish(self):
            for copy in [self.from_chan()] + self.samp_gather(False) + self.x_gather(False) + self.core_gather(False):
                copy.wait_send()

    ones = [Filter(0, wall1, k) for k in range(1, nc)]
    twos = [Filter(1, wall2, k) for k in range(1, nc)]

    for wall, w_ref in ((wall1, w1_ref), (wall2, w2_ref)):
        wall[ci, 0 : 27 * n, :] = w_ref[...].reshape(27 * n, channels)
        if ns * shard > 27 * n:
            wall[ci, 27 * n : ns * shard, :] = jnp.zeros((ns * shard - 27 * n, channels), BF16)
    for item in ones + twos:
        item.zero()
    for d in range(planes):
        xpad[1 + d, own, :] = to_blocks(x_ref[d])
    for copy in gather_sends(xpad, sx, rx):
        copy.start()
    start_halo(xpad, own, sxh, rxh, 0)
    for d in range(planes):
        ctpad[1 + d, own, :] = to_blocks(ct_ref[d])
    for copy in gather_sends(ctpad, sct, rct):
        copy.start()
    start_halo(ctpad, own, scth, rcth, 0)
    zero_edges(xpad)
    zero_edges(ctpad)
    zero_edges(hpad)
    zero_edges(gppad)
    lay_forward(fw2, lambda tap: w2_ref[tap])
    for item in ones + twos:
        item.one()
    for item in ones + twos:
        item.two()
    gather_and_forward(xpad, sx, rx, sxh, rxh)
    for plane in range(1, planes + 1):
        build(wide, xpad, plane)
    for item in ones + twos:
        item.three()
    for k in range(nc):
        wait_halo(xpad, rows_of(lax.rem(ci + nc - k, nc)), sxh, rxh, k)
    build(wide, xpad, 0)
    build(wide, xpad, planes + 1)
    for item in ones:
        item.four()
    lay_forward(fw1, all_outputs(wall1))

    def hidden_out(d, cols, total):
        pre[d, :, cols] = total
        hpad[d + 1, :, cols] = (total * jax.nn.sigmoid(total)).astype(BF16)

    convolve(lambda a: fw1[a], channels, wide, hidden_out)
    start_halo(hpad, everything, shh, rhh, 0)
    gather_and_forward(ctpad, sct, rct, scth, rcth)
    for plane in range(1, planes + 1):
        build(st_ct, ctpad, plane, -1)
    wait_halo(hpad, everything, shh, rhh, 0)
    filter_grad(g2, st_ct, hpad)
    second.one()
    for item in twos:
        item.four()
    lay_backward(bw2, all_outputs(wall2))
    for k in range(nc):
        wait_halo(ctpad, rows_of(lax.rem(ci + nc - k, nc)), scth, rcth, k)
    build(st_ct, ctpad, 0, -1)
    build(st_ct, ctpad, planes + 1, -1)
    second.two()

    def slope(d, cols, total):
        values = pre[d, :, cols]
        sigma = jax.nn.sigmoid(values)
        gppad[d + 1, :, cols] = (total * (sigma * (1.0 + values * (1.0 - sigma)))).astype(BF16)

    convolve(lambda a: bw2[a], channels, st_ct, slope, reverse=True)
    start_halo(gppad, everything, sgp, rgp, 0)
    for plane in range(1, planes + 1):
        build(st_gp, gppad, plane, -1)
    second.three()
    filter_grad(g1, st_gp, xpad)
    first.one()
    lay_backward(bw1, all_outputs(wall1))
    second.four()
    first.two()
    for plane in range(planes + 2):
        build(wide, hpad, plane)
    second.five()
    first.three()

    def block(d, cols, total):
        result[d, :, cols] = (xpad[1 + d, own, cols].astype(F32) + total).astype(BF16)

    convolve(lambda a: fw2[a], n, wide, block)
    second.six()
    first.four()
    for d in range(planes):
        out_ref[d] = from_blocks(result[d])
    wait_halo(gppad, everything, sgp, rgp, 0)
    build(st_gp, gppad, 0, -1)
    build(st_gp, gppad, planes + 1, -1)
    first.five()

    def volume_grad(d, cols, total):
        result[d, :, cols] = (ctpad[1 + d, own, cols].astype(F32) + total).astype(BF16)

    convolve(lambda a: bw1[a, own, :], n, st_gp, volume_grad, reverse=True)
    first.six()
    for d in range(planes):
        gv_ref[d] = from_blocks(result[d])
    second.seven()
    first.seven()

    for copy in gather_sends(xpad, sx, rx) + gather_sends(ctpad, sct, rct):
        copy.wait_send()
    for k in range(nc):
        rows = rows_of(lax.rem(ci + nc - k, nc))
        finish_halo(xpad, rows, sxh, rxh, k)
        finish_halo(ctpad, rows, scth, rcth, k)
    finish_halo(hpad, everything, shh, rhh, 0)
    finish_halo(gppad, everything, sgp, rgp, 0)
    for item in ones + twos + [first, second]:
        item.finish()


def per_device(volume, cotangent, filter_one, filter_two):
    n, planes, cells = volume.shape[1:]
    nz, ns, nc = (lax.axis_size(axis) for axis in ("samp", "slab", "chan"))
    channels = n * nc
    norm_scale = 1.0 / math.sqrt(nz * planes * ns * cells)
    unit = 16 * ns * nz
    rows = -(-27 * n // unit) * unit
    shard, piece = rows // ns, rows // ns // nz

    def by_tap(weight):
        return jnp.transpose(weight, (1, 0, 2))

    x = jnp.transpose(volume[0], (1, 0, 2))
    ct = jnp.transpose(cotangent[0], (1, 0, 2))
    vmem = pl.BlockSpec(memory_space=pltpu.VMEM)
    padded = planes + 2
    dma = pltpu.SemaphoreType.DMA

    nx = ns // 2

    def reduction_buffers(dtypes):
        one, two, three = dtypes
        return [pltpu.VMEM((nx * shard, channels), one)] * 2 + [
            pltpu.VMEM((nx - 1, shard, channels), two)] * 2 + [
            pltpu.VMEM((nz - 1, piece, channels), three)] * 2

    stack = pltpu.VMEM((padded, 9 * channels, cells), BF16)
    plane_buffer = pltpu.VMEM((padded, channels, cells), BF16)
    scratch = [
        pltpu.VMEM((3, channels, 9 * channels), BF16),
        pltpu.VMEM((3, n, 9 * channels), BF16),
        pltpu.VMEM((3, channels, 9 * channels), BF16),
        pltpu.VMEM((3, channels, 9 * channels), BF16),
        pltpu.VMEM((nc, rows, channels), BF16),
        pltpu.VMEM((nc, rows, channels), BF16),
        pltpu.VMEM((planes, n, cells), BF16),
        plane_buffer, plane_buffer, plane_buffer, plane_buffer, stack, stack, stack,
        pltpu.VMEM((planes, channels, cells), F32),
        pltpu.VMEM((rows, channels), F32),
        pltpu.VMEM((rows, channels), F32),
        reduction_buffers(SUM_TYPES[0]),
        reduction_buffers(SUM_TYPES[1]),
        dma((planes * nc,)), dma((planes * nc,)), dma((2 * nc,)), dma((2 * nc,)),
        dma((planes * nc,)), dma((planes * nc,)), dma((2 * nc,)), dma((2 * nc,)),
        dma((2,)), dma((2,)), dma((2,)), dma((2,)),
        dma((2 * nc * (3 + ns + nz),)), dma((2 * nc * (3 + ns + nz),)),
        dma((4 * (1 + ns + nz),)), dma((4 * (1 + ns + nz),)),
    ]
    sizes = (nz, ns, nc, n, planes, shard, piece, norm_scale)
    block, grad_volume, one, two = pl.pallas_call(
        functools.partial(kernel, sizes),
        out_shape=(
            jax.ShapeDtypeStruct((planes, n, cells), BF16),
            jax.ShapeDtypeStruct((planes, n, cells), BF16),
            jax.ShapeDtypeStruct((rows, channels), BF16),
            jax.ShapeDtypeStruct((rows, channels), BF16),
        ),
        in_specs=[vmem] * 4,
        out_specs=(vmem,) * 4,
        scratch_shapes=scratch,
        compiler_params=pltpu.CompilerParams(
            collective_id=0, has_side_effects=True, vmem_limit_bytes=56 * 1024 * 1024),
        cost_estimate=pl.CostEstimate(
            flops=6 * 2 * planes * cells * n * 27 * channels, bytes_accessed=8 << 20, transcendentals=planes * n * cells),
        name="residual_pair",
    )(x, ct, by_tap(filter_one), by_tap(filter_two))

    def filter_out(values):
        values = values[: 27 * n].reshape(3, 9, n, channels)
        return jnp.transpose(values, (2, 0, 1, 3)).reshape(n, 27, channels).astype(F32)

    return (
        jnp.transpose(block, (1, 0, 2))[None],
        jnp.transpose(grad_volume, (1, 0, 2))[None],
        filter_out(one),
        filter_out(two),
    )


def solution(mesh):
    return jax.shard_map(
        per_device,
        mesh=mesh,
        in_specs=(
            P("samp", "chan", "slab", None),
            P("samp", "chan", "slab", None),
            P("chan", None, None),
            P("chan", None, None),
        ),
        out_specs=(
            P("samp", "chan", "slab", None),
            P("samp", "chan", "slab", None),
            P("chan", None, None),
            P("chan", None, None),
        ),
        check_vma=False,
    )
```
